32 devices in a mesh: seq: 8 (over y, x, core), kv: 4 (over z).
Axes of the slice: x: 2, y: 2, z: 4, core: 2. Of those that a mesh axis runs over, the one named last changes fastest.
Arguments:
- activations: bfloat16 [2, 2048, 2048], P(None, 'seq'), may hold values from -6 to 6
- cotangent: bfloat16 [2, 2048, 2048], P(None, 'seq'), may hold values from -6 to 6
- document_starts: int32 [2, 4], replicated, may hold values from 0 to 2048, as said below
- norm_gain_pair: bfloat16 [2, 2048], P(None, 'seq'), may hold values from 0.5 to 1.5
- query_projection_weight: bfloat16 [2048, 2048], P('seq', 'kv'), may hold values from -0.125 to 0.125
- key_value_weight: bfloat16 [2, 2048, 512], P(None, 'seq', 'kv'), may hold values from -0.125 to 0.125
- output_projection_weight: bfloat16 [2048, 2048], P('kv', 'seq'), may hold values from -0.5 to 0.5
- gate_up_weight: bfloat16 [2, 2048, 8192], P(None, 'seq', 'kv'), may hold values from -0.125 to 0.125
- down_weight: bfloat16 [8192, 2048], P('kv', 'seq'), may hold values from -0.0625 to 0.0625
- adapter_down_maps: bfloat16 [2048, 24], P('seq'), may hold values from -0.125 to 0.125
- query_adapter_up: bfloat16 [8, 2048], P(None, 'kv'), may hold values from -1 to 1
- keyval_adapter_up: bfloat16 [2, 8, 512], P(None, None, 'kv'), may hold values from -1 to 1
- output_adapter_down: bfloat16 [2048, 8], P('kv'), may hold values from -1 to 1
- output_adapter_up: bfloat16 [8, 2048], P(None, 'seq'), may hold values from -2 to 2
- hedgehog_maps: float32 [2, 32, 64, 64], P(None, 'kv'), may hold values from -0.75 to 0.75
Outputs:
- block_out: bfloat16 [2, 2048, 2048], P(None, 'seq', 'kv')
- grad_input: float32 [2, 2048, 2048], P(None, 'seq')
- grad_gains: float32 [2, 2048], P(None, 'seq')
- grad_query: float32 [2048, 2048], P('seq', 'kv')
- grad_keyval: float32 [2, 2048, 512], P(None, 'seq', 'kv')
- grad_project: float32 [2048, 2048], P('kv', 'seq')
- grad_gateup: float32 [2, 2048, 8192], P(None, 'seq', 'kv')
- grad_down: float32 [8192, 2048], P('kv', 'seq')
- grad_enter: float32 [2048, 24], P('seq')
- grad_lora_query: float32 [8, 2048], P(None, 'kv')
- grad_lora_keyval: float32 [2, 8, 512], P(None, None, 'kv')
- grad_reduce: float32 [2048, 8], P('kv')
- grad_expand: float32 [8, 2048], P(None, 'seq')
- grad_maps: float32 [2, 32, 64, 64], P(None, 'kv')
The draws below stay inside these ranges and needn't reach their ends.
Inputs may be any that keep to these rules, and one draw needn't show every extreme that they name: `document_starts`: each row never falls and begins with 0; an entry equal to 2048 opens an empty document at the end. In one micro-batch, drawn from the seed, the row is 0 followed by 2048 only: one document spans all its tokens. Every document that is not empty has 1024 tokens or more.
All inputs are finite; a program needn't handle non-finite values.
Results may differ from the reference program's by a relative error of at most 0.02.
Values may be sent and summed in bfloat16 or wider, within the bound.
No kernel may reach another device: no remote copies, remote signals or barrier semaphores. Data moves between devices by JAX's collectives and lax.ppermute only.
A program may use at most 384 MiB of HBM per device.

```python
import jax
import jax.numpy as jnp
from jax import lax

MODEL_WIDTH = 2048
QUERY_HEADS = 32
KEY_HEADS = 8
HEAD_SIZE = 64
FF = 8192
ADAPTER_RANK = 8
WIN = 64
MICRO_TOKENS = 256
MB = 2
DOCS = 4
SEGLEN = 2048
TOKENS = 2048


def draw_document_starts(key, part):
    unit_count = TOKENS // SEGLEN
    cut_count = min(DOCS - 1, unit_count - 1)
    whole_key, cut_key = jax.random.split(key)
    whole_index = jax.random.randint(whole_key, (), 0, MB)
    drawn = jnp.concatenate([jnp.zeros((1,), jnp.int32), jnp.full((DOCS - 1,), TOKENS, jnp.int32)])
    starts_rows = []
    for batch_index in range(MB):
        row_key = jax.random.fold_in(cut_key, batch_index)
        pick_key, shift_key = jax.random.split(row_key)
        if cut_count > 0:
            chosen = jnp.sort(jax.random.permutation(pick_key, unit_count - 1)[:cut_count] + 1)
            jitter = jax.random.randint(shift_key, (cut_count,), 0, SEGLEN // 2)
            cut_points = (chosen * SEGLEN + jitter).astype(jnp.int32)
        else:
            cut_points = jnp.zeros((0,), jnp.int32)
        padding = jnp.full((DOCS - 1 - cut_count,), TOKENS, jnp.int32)
        ragged = jnp.concatenate([jnp.zeros((1,), jnp.int32), cut_points, padding])
        starts_rows.append(jnp.where(whole_index == batch_index, drawn, ragged))
    return jnp.stack(starts_rows).astype(jnp.int32)


def shard_levels(key, dims, cuts, low, high):
    def one(axis_at, shards_of):
        heights = jax.random.uniform(jax.random.fold_in(jax.random.fold_in(key, 6), axis_at), (shards_of,), jnp.float32, low / len(cuts), high / len(cuts))
        return jnp.repeat(jnp.exp(heights), dims[axis_at] // shards_of).reshape((-1,) + (1,) * (len(dims) - axis_at - 1))

    factor_of = one(*cuts[0])
    for cut in cuts[1:]:
        factor_of = factor_of * one(*cut)
    return factor_of


def centred(stream_key, extent, width, most, cuts=(), held_as=jnp.bfloat16):
    array = width * jax.random.normal(stream_key, extent, jnp.float32)
    if cuts:
        array = array * shard_levels(stream_key, extent, cuts, -0.22, 0.18)
    return jnp.clip(array, -most, most).astype(held_as)


def setup_inputs(seed: int = 0) -> dict:
    key_list = jax.random.split(jax.random.key(seed), 16)
    activations = centred(key_list[0], (MB, TOKENS, MODEL_WIDTH), 1.0, 6.0, ((1, 8),))
    cotangent = centred(key_list[1], (MB, TOKENS, MODEL_WIDTH), 1.0, 6.0, ((1, 8),))
    document_starts = draw_document_starts(jax.random.fold_in(key_list[15], 71), 0)
    norm_gain_pair = jnp.clip(1.0 + 0.1 * jax.random.normal(key_list[3], (2, MODEL_WIDTH), jnp.float32), 0.5, 1.5).astype(jnp.bfloat16)
    query_projection_weight = centred(key_list[4], (MODEL_WIDTH, QUERY_HEADS * HEAD_SIZE), MODEL_WIDTH ** -0.5, 0.125, ((0, 8), (1, 4)))
    key_value_weight = centred(key_list[5], (2, MODEL_WIDTH, KEY_HEADS * HEAD_SIZE), MODEL_WIDTH ** -0.5, 0.125, ((1, 8), (2, 4)))
    output_projection_weight = centred(key_list[6], (QUERY_HEADS * HEAD_SIZE, MODEL_WIDTH), (QUERY_HEADS * HEAD_SIZE // 16) ** -0.5, 0.5, ((0, 4), (1, 8)))
    gate_up_weight = centred(key_list[7], (2, MODEL_WIDTH, FF), MODEL_WIDTH ** -0.5, 0.125, ((1, 8), (2, 4)))
    down_weight = centred(key_list[8], (FF, MODEL_WIDTH), FF ** -0.5, 0.0625, ((0, 4), (1, 8)))
    adapter_down_maps = centred(key_list[9], (MODEL_WIDTH, 3 * ADAPTER_RANK), MODEL_WIDTH ** -0.5, 0.125, ((0, 8),))
    query_adapter_up = centred(key_list[10], (ADAPTER_RANK, QUERY_HEADS * HEAD_SIZE), (4 * ADAPTER_RANK) ** -0.5, 1.0, ((1, 4),))
    keyval_adapter_up = centred(key_list[11], (2, ADAPTER_RANK, KEY_HEADS * HEAD_SIZE), (4 * ADAPTER_RANK) ** -0.5, 1.0, ((2, 4),))
    output_adapter_down = centred(key_list[12], (QUERY_HEADS * HEAD_SIZE, ADAPTER_RANK), (QUERY_HEADS * HEAD_SIZE // 64) ** -0.5, 1.0, ((0, 4),))
    output_adapter_up = centred(key_list[13], (ADAPTER_RANK, MODEL_WIDTH), ADAPTER_RANK ** -0.5, 2.0, ((1, 8),))
    hedgehog_maps = centred(key_list[14], (2, QUERY_HEADS, HEAD_SIZE, HEAD_SIZE), HEAD_SIZE ** -0.5, 0.75, ((1, 4),), jnp.float32)
    return {"activations": activations, "cotangent": cotangent, "document_starts": document_starts, "norm_gain_pair": norm_gain_pair, "query_projection_weight": query_projection_weight, "key_value_weight": key_value_weight, "output_projection_weight": output_projection_weight, "gate_up_weight": gate_up_weight, "down_weight": down_weight, "adapter_down_maps": adapter_down_maps, "query_adapter_up": query_adapter_up, "keyval_adapter_up": keyval_adapter_up, "output_adapter_down": output_adapter_down, "output_adapter_up": output_adapter_up, "hedgehog_maps": hedgehog_maps}


EPSILON = 1e-05
EXACT_MODE = lax.Precision.HIGHEST

@jax.custom_vjp
def low(v):
    return lax.optimization_barrier(v.astype(jnp.bfloat16)).astype(jnp.float32)

@jax.custom_vjp
def low_back(v):
    return v

def low_keep(v):
    return (low(v), None)

def low_pass(kept, grad):
    return (grad,)

def back_keep(v):
    return (v, None)

def back_low(kept, grad):
    return (low(grad),)
low.defvjp(low_keep, low_pass)
low_back.defvjp(back_keep, back_low)

def matmul(left, right):
    return jnp.dot(left, right, precision=EXACT_MODE)

def doc_of(starts, positions):
    counted = lax.optimization_barrier(jnp.sum((starts[None, :] <= positions[:, None]).astype(jnp.int32), axis=1, dtype=jnp.int32))
    return (counted - 1).astype(jnp.int32)

def feature(values, maps):
    projected = jnp.einsum('rhd,hde->rhe', values, maps, precision=EXACT_MODE)
    return jnp.concatenate([jax.nn.softmax(projected, axis=-1), jax.nn.softmax(-projected, axis=-1)], axis=-1)

def rms_scale(values):
    return lax.rsqrt(lax.optimization_barrier(jnp.mean(values * values, axis=-1, keepdims=True)) + EPSILON)

def local_block(query_blk, key_blk, value_block, maps, previous_state, norm_prev, doc_prev, begin, starts):
    pos_query = begin + jnp.arange(MICRO_TOKENS, dtype=jnp.int32)
    pos_key = begin - WIN + jnp.arange(MICRO_TOKENS + WIN, dtype=jnp.int32)
    doc_query = doc_of(starts, pos_query)
    doc_key = doc_of(starts, pos_key)
    gap_size = pos_query[:, None] - pos_key[None, :]
    same_doc = doc_query[:, None] == doc_key[None, :]
    near_mask = same_doc & (gap_size >= 0) & (gap_size < WIN)
    distant_mask = same_doc & (gap_size >= WIN)
    scores = jnp.einsum('qhd,khd->hqk', query_blk, key_blk, precision=EXACT_MODE) * HEAD_SIZE ** (-0.5)
    expo_terms = jnp.where(near_mask[None], jnp.exp(scores), 0.0)
    feature_query = feature(query_blk, maps[0])
    feature_key = feature(key_blk, maps[1])
    linear_parts = jnp.where(distant_mask[None], jnp.einsum('ain,pin->iap', feature_query, feature_key, precision=EXACT_MODE), 0.0)
    use_state = (doc_query == doc_prev).astype(jnp.float32)
    numerator = jnp.einsum('hqk,khd->qhd', low(expo_terms), value_block, precision=EXACT_MODE) + jnp.einsum('hqk,khd->qhd', linear_parts, value_block, precision=EXACT_MODE) + use_state[:, None, None] * jnp.einsum('qhf,hfd->qhd', feature_query, previous_state, precision=EXACT_MODE)
    denominator = lax.optimization_barrier(jnp.sum(expo_terms, axis=-1)) + lax.optimization_barrier(jnp.sum(linear_parts, axis=-1)) + use_state[None, :] * jnp.einsum('qhf,hf->hq', feature_query, norm_prev, precision=EXACT_MODE)
    attended = numerator / jnp.transpose(denominator)[:, :, None]
    last_doc = doc_key[MICRO_TOKENS - 1].astype(jnp.int32)
    keep_mask = (doc_key[:MICRO_TOKENS] == last_doc).astype(jnp.float32)
    carry_onward = (last_doc == doc_prev).astype(jnp.float32)
    masked_scores = feature_key[:MICRO_TOKENS] * keep_mask[:, None, None]
    following_state = carry_onward * previous_state + jnp.einsum('pae,pat->aet', masked_scores, value_block[:MICRO_TOKENS], precision=EXACT_MODE)
    norm_next = carry_onward * norm_prev + lax.optimization_barrier(jnp.sum(masked_scores, axis=0))
    return (attended, following_state, norm_next, last_doc)

def attention(query_all, key_all, value_all, maps, starts):
    group_size = QUERY_HEADS // KEY_HEADS
    key_rep = jnp.repeat(key_all, group_size, axis=1)
    value_repeated = jnp.repeat(value_all, group_size, axis=1)
    padding = jnp.zeros((WIN, QUERY_HEADS, HEAD_SIZE), jnp.float32)
    key_pad = jnp.concatenate([padding, key_rep], axis=0)
    value_pad = jnp.concatenate([padding, value_repeated], axis=0)

    def block_step(carry, block_index):
        previous_state, norm_prev, doc_prev = carry
        begin = (block_index * MICRO_TOKENS).astype(jnp.int32)
        query_blk = lax.dynamic_slice_in_dim(query_all, begin, MICRO_TOKENS, 0)
        key_blk = lax.dynamic_slice_in_dim(key_pad, begin, MICRO_TOKENS + WIN, 0)
        value_block = lax.dynamic_slice_in_dim(value_pad, begin, MICRO_TOKENS + WIN, 0)
        attended, following_state, norm_next, last_doc = local_block(query_blk, key_blk, value_block, maps, previous_state, norm_prev, doc_prev, begin, starts)
        return ((following_state, norm_next, last_doc), attended)
    initial = (jnp.zeros((QUERY_HEADS, 2 * HEAD_SIZE, HEAD_SIZE), jnp.float32), jnp.zeros((QUERY_HEADS, 2 * HEAD_SIZE), jnp.float32), jnp.int32(-1))
    block_count = TOKENS // MICRO_TOKENS
    unused_carry, blocks = lax.scan(jax.checkpoint(block_step), initial, jnp.arange(block_count, dtype=jnp.int32))
    return blocks.reshape(TOKENS, QUERY_HEADS * HEAD_SIZE)

def feed_forward(resid, gain_two, gateup_w, down_w):
    normed_two = low(resid * rms_scale(resid) * gain_two)
    gate = low_back(matmul(normed_two, gateup_w[0]))
    upper = low_back(matmul(normed_two, gateup_w[1]))
    hidden = low(jax.nn.silu(gate) * upper)
    return low_back(matmul(hidden, down_w))

def layer_forward(inputs_f, starts, gains, query_weight, keyval_weight, projection_weight, gateup_w, down_w, enter_w, adapt_query, adapt_keyval, adapt_reduce, adapt_expand, maps):
    first_normed = low(inputs_f * rms_scale(inputs_f) * gains[0])
    adapter_apply = low(matmul(first_normed, enter_w))
    query_all = low_back(low(matmul(first_normed, query_weight) + matmul(adapter_apply[:, :ADAPTER_RANK], adapt_query)))
    key_all = low_back(low(matmul(first_normed, keyval_weight[0]) + matmul(adapter_apply[:, ADAPTER_RANK:2 * ADAPTER_RANK], adapt_keyval[0])))
    value_all = low_back(low(matmul(first_normed, keyval_weight[1]) + matmul(adapter_apply[:, 2 * ADAPTER_RANK:], adapt_keyval[1])))
    attended = attention(query_all.reshape(TOKENS, QUERY_HEADS, HEAD_SIZE), key_all.reshape(TOKENS, KEY_HEADS, HEAD_SIZE), value_all.reshape(TOKENS, KEY_HEADS, HEAD_SIZE), maps, starts)
    attended = low_back(low(attended))
    reduced = low(matmul(attended, adapt_reduce))
    resid = inputs_f + low_back(matmul(attended, projection_weight) + matmul(reduced, adapt_expand))
    return resid + jax.checkpoint(feed_forward)(resid, gains[1], gateup_w, down_w)

def reference(activations, cotangent, document_starts, norm_gain_pair, query_projection_weight, key_value_weight, output_projection_weight, gate_up_weight, down_weight, adapter_down_maps, query_adapter_up, keyval_adapter_up, output_adapter_down, output_adapter_up, hedgehog_maps):
    parameters = tuple((argument_value.astype(jnp.float32) for argument_value in (norm_gain_pair, query_projection_weight, key_value_weight, output_projection_weight, gate_up_weight, down_weight, adapter_down_maps, query_adapter_up, keyval_adapter_up, output_adapter_down, output_adapter_up, hedgehog_maps)))
    outputs = []
    grad_inputs = []
    totals = None
    for batch_index in range(MB):
        starts = document_starts[batch_index].astype(jnp.int32)

        def forward(inputs_f, *weights):
            return layer_forward(inputs_f, starts, *weights)
        result, pull_back = jax.vjp(forward, activations[batch_index].astype(jnp.float32), *parameters)
        gradients = pull_back(cotangent[batch_index].astype(jnp.float32))
        outputs.append(result.astype(jnp.bfloat16))
        grad_inputs.append(gradients[0])
        if totals is None:
            totals = gradients[1:]
        else:
            totals = tuple((total + extra for total, extra in zip(totals, gradients[1:])))
    return (jnp.stack(outputs), jnp.stack(grad_inputs), totals[0], totals[1], totals[2], totals[3], totals[4], totals[5], totals[6], totals[7], totals[8], totals[9], totals[10], totals[11])
```

```python
import functools

import jax
import jax.numpy as jnp
from jax import lax
from jax.experimental import pallas as pl
from jax.experimental.pallas import tpu as pltpu
from jax.sharding import PartitionSpec as P

MODEL_WIDTH = 2048
HEAD_SIZE = 64
ADAPTER_RANK = 8
WIN = 64
MB = 2
EPSILON = 1e-05
AUG = 80
F32 = jnp.float32
BF16 = jnp.bfloat16
VMEM_LIMIT = 56 * 1024 * 1024


def contract(left, right, dims):
    return lax.dot_general(left, right, (dims, ((), ())), preferred_element_type=F32)


def nn(left, right):
    return contract(left, right, ((1,), (0,)))


def nt(left, right):
    return contract(left, right, ((1,), (1,)))


def tn(left, right):
    return contract(left, right, ((0,), (0,)))


def cost(micros):
    return pl.CostEstimate(flops=int(micros * 1.1e9), bytes_accessed=1 << 20, transcendentals=0)


def params(count):
    return pltpu.CompilerParams(
        dimension_semantics=("arbitrary",) * count, vmem_limit_bytes=VMEM_LIMIT
    )


def flip(value, axis, bit):
    count = lax.axis_size(axis)
    return lax.ppermute(value, axis, [(i, i ^ bit) for i in range(count)])


def shift(value, axis, steps):
    count = lax.axis_size(axis)
    first, last = max(0, -steps), min(count, count - steps)
    return lax.ppermute(value, axis, [(i, i + steps) for i in range(first, last)])


def sum_all(value, axis):
    count = lax.axis_size(axis)
    value = value.astype(F32)
    for k in range(count.bit_length() - 1):
        narrow = value.astype(BF16)
        value = narrow.astype(F32) + flip(narrow, axis, 1 << k).astype(F32)
    return value


def sum_once(value, axis):
    count = lax.axis_size(axis)
    narrow = value.astype(BF16)
    terms = [narrow.astype(F32)] + [flip(narrow, axis, k).astype(F32) for k in range(1, count)]
    while len(terms) > 1:
        terms = [terms[k] + terms[k + 1] for k in range(0, len(terms), 2)]
    return terms[0]


def together(*values):
    return lax.optimization_barrier(values)


def scatter_lanes(value, axis):
    count, me = lax.axis_size(axis), lax.axis_index(axis)
    bit = count // 2
    while bit:
        cut = value.shape[1] // 2
        high = (me & bit) != 0
        kept = jnp.where(high, value[:, cut:], value[:, :cut])
        sent = jnp.where(high, value[:, :cut], value[:, cut:])
        value = kept + flip(sent.astype(BF16), axis, bit).astype(F32)
        bit //= 2
    return value


def level_send(pieces, dim):
    count, level = lax.axis_size("kv"), lax.axis_index("kv")
    terms = [lax.dynamic_index_in_dim(pieces, level, dim, keepdims=False)]
    for k in range(1, count):
        sent = lax.dynamic_index_in_dim(pieces, level ^ k, dim, keepdims=False)
        terms.append(flip(sent, "kv", k))
    return terms


def total_of(terms):
    total = terms[0].astype(F32)
    for term in terms[1:]:
        total = total + term.astype(F32)
    return total


def level_spread(own):
    count = lax.axis_size("kv")
    return [own] + [flip(own, "kv", k) for k in range(1, count)]


def level_rows(pieces, dtype, gain=None):
    count, level = lax.axis_size("kv"), lax.axis_index("kv")
    m, rows, width = pieces[0].shape
    gains = [] if gain is None else [gain]

    def kernel(level_ref, *refs):
        out_ref = refs[count + len(gains)]
        for k in range(count):
            at = pl.multiple_of((level_ref[0] ^ k) * rows, rows)
            for b in range(m):
                value = refs[k][b]
                out_ref[b, pl.ds(at, rows), :] = value.astype(dtype)
                if gains:
                    wide = value.astype(F32)
                    scale = lax.rsqrt(jnp.mean(wide * wide, axis=1, keepdims=True) + EPSILON)
                    refs[-1][b, pl.ds(at, rows), :] = (wide * scale * refs[count][...]).astype(BF16)

    whole = pl.BlockSpec(memory_space=pltpu.VMEM)
    shape = (m, rows * count, width)
    found = pl.pallas_call(
        kernel,
        in_specs=[pl.BlockSpec(memory_space=pltpu.SMEM)] + [whole] * (count + len(gains)),
        out_specs=[whole] * (1 + len(gains)),
        out_shape=[jax.ShapeDtypeStruct(shape, dtype)]
        + [jax.ShapeDtypeStruct(shape, BF16)] * len(gains),
        compiler_params=pltpu.CompilerParams(vmem_limit_bytes=VMEM_LIMIT),
    )(jnp.reshape(level, (1,)), *pieces, *gains)
    found = [part.reshape(m * rows * count, width) for part in found]
    return found if gains else found[0]


def first_hops(shard):
    return [shard] + [flip(shard, "seq", k) for k in range(2, lax.axis_size("seq"), 2)]


def second_hops(own):
    other = [flip(piece, "seq", 1) for piece in own]
    return [piece for pair in zip(own, other) for piece in pair]


def ordered_rows(pieces):
    count, me = lax.axis_size("seq"), lax.axis_index("seq")
    rows, width = pieces[0].shape

    def kernel(me_ref, *refs):
        out_ref = refs[-1]
        for k in range(count):
            out_ref[pl.ds(pl.multiple_of((me_ref[0] ^ k) * rows, rows), rows), :] = refs[k][...]

    whole = pl.BlockSpec(memory_space=pltpu.VMEM)
    return pl.pallas_call(
        kernel,
        in_specs=[pl.BlockSpec(memory_space=pltpu.SMEM)] + [whole] * count,
        out_specs=whole,
        out_shape=jax.ShapeDtypeStruct((rows * count, width), pieces[0].dtype),
        compiler_params=pltpu.CompilerParams(vmem_limit_bytes=VMEM_LIMIT),
    )(jnp.reshape(me, (1,)), *pieces)


def parity_rows(left, parity):
    count = lax.axis_size("seq")
    view = left.reshape(left.shape[0], count // 2, 2, left.shape[1] // count)
    return lax.dynamic_index_in_dim(view, parity, 2, keepdims=False).reshape(left.shape[0], -1)


def chip_pair(kept, arrived):
    count, me = lax.axis_size("seq"), lax.axis_index("seq")
    pair = (kept.astype(F32) + arrived.astype(F32)).astype(BF16)
    pair = pair.reshape(count // 2, -1, pair.shape[1])
    chip = me // 2
    terms = [lax.dynamic_index_in_dim(pair, chip, 0, keepdims=False)]
    for k in range(1, count // 2):
        sent = lax.dynamic_index_in_dim(pair, chip ^ k, 0, keepdims=False)
        terms.append(flip(sent, "seq", 2 * k))
    return terms


def wide_gradients(normed, d_gu, cotangents, hidden):
    rows, width = normed.shape
    tile = 256
    first, second = d_gu.shape[1] // tile, hidden.shape[1] // tile

    def kernel(n_ref, dgu_ref, c_ref, h_ref, out_ref, left_ref):
        t = pl.program_id(0)

        @pl.when(t == 0)
        def _():
            left_ref[...] = n_ref[...].T

        @pl.when(t == first)
        def _():
            left_ref[...] = c_ref[...].T

        right = jnp.where(t < first, dgu_ref[...], h_ref[...])
        out_ref[...] = nn(left_ref[...], right).astype(BF16)

    return pl.pallas_call(
        kernel,
        grid=(first + second,),
        in_specs=[
            pl.BlockSpec((rows, width), lambda t: (0, 0)),
            pl.BlockSpec((rows, tile), lambda t: (0, jnp.minimum(t, first - 1))),
            pl.BlockSpec((rows, width), lambda t: (0, 0)),
            pl.BlockSpec((rows, tile), lambda t: (0, jnp.maximum(t - first, 0))),
        ],
        out_specs=pl.BlockSpec((width, tile), lambda t: (0, t)),
        out_shape=jax.ShapeDtypeStruct((width, (first + second) * tile), BF16),
        scratch_shapes=[pltpu.VMEM((width, rows), BF16)],
        compiler_params=params(1),
        cost_estimate=cost(20),
    )(normed, d_gu, cotangents, hidden)


def feed_forward(normed, d_hidden, gate_up):
    rows, width = normed.shape
    units = gate_up.shape[1] // 2
    tile = 256
    steps = units // tile

    def kernel(n_ref, dh_ref, g_ref, u_ref, hidden_ref, dgu_ref, dn_ref, acc_ref):
        t = pl.program_id(0)
        gate = nn(n_ref[...], g_ref[...])
        upper = nn(n_ref[...], u_ref[...])
        sigma = jax.nn.sigmoid(gate)
        silu = gate * sigma
        hidden_ref[...] = (silu * upper).astype(BF16)
        d_hid = dh_ref[...].astype(F32)
        d_gate = (d_hid * upper * (sigma * (1.0 + gate * (1.0 - sigma)))).astype(BF16)
        d_upper = (d_hid * silu).astype(BF16)
        at = pl.multiple_of(t * tile, tile)
        dgu_ref[:, pl.ds(at, tile)] = d_gate
        dgu_ref[:, pl.ds(units + at, tile)] = d_upper
        part = nt(d_gate, g_ref[...]) + nt(d_upper, u_ref[...])

        @pl.when(t == 0)
        def _():
            acc_ref[...] = part

        @pl.when(t > 0)
        def _():
            acc_ref[...] += part

        @pl.when(t == steps - 1)
        def _():
            dn_ref[...] = acc_ref[...].astype(BF16)

    return pl.pallas_call(
        kernel,
        grid=(steps,),
        in_specs=[
            pl.BlockSpec((rows, width), lambda t: (0, 0)),
            pl.BlockSpec((rows, tile), lambda t: (0, t)),
            pl.BlockSpec((width, tile), lambda t: (0, t)),
            pl.BlockSpec((width, tile), lambda t: (0, t + steps)),
        ],
        out_specs=[
            pl.BlockSpec((rows, tile), lambda t: (0, t)),
            pl.BlockSpec((rows, 2 * units), lambda t: (0, 0)),
            pl.BlockSpec((rows, width), lambda t: (0, 0)),
        ],
        out_shape=[
            jax.ShapeDtypeStruct((rows, units), BF16),
            jax.ShapeDtypeStruct((rows, 2 * units), BF16),
            jax.ShapeDtypeStruct((rows, width), BF16),
        ],
        scratch_shapes=[pltpu.VMEM((rows, width), F32)],
        compiler_params=params(1),
        cost_estimate=cost(29),
    )(normed, d_hidden, gate_up, gate_up)


def masks(doc_q, doc_k, stretch):
    keys = stretch + WIN
    row = lax.broadcasted_iota(jnp.int32, (keys, stretch), 0)
    place = jnp.where(row < stretch, row, row - keys)
    gap = lax.broadcasted_iota(jnp.int32, (keys, stretch), 1) - place
    same = doc_k == doc_q
    near = same & (gap >= 0) & (gap < WIN)
    far = same & (gap >= WIN)
    return near, far


def soft_pair(projected):
    one = jnp.exp(projected - jnp.max(projected, axis=0, keepdims=True))
    two = jnp.exp(jnp.min(projected, axis=0, keepdims=True) - projected)
    one = one * (1.0 / jnp.sum(one, axis=0, keepdims=True))
    two = two * (1.0 / jnp.sum(two, axis=0, keepdims=True))
    return jnp.concatenate([one, two], axis=0).astype(BF16)


def soft_pair_back(feat, grad):
    s1, s2 = feat[:HEAD_SIZE].astype(F32), feat[HEAD_SIZE:].astype(F32)
    t1, t2 = s1 * grad[:HEAD_SIZE], s2 * grad[HEAD_SIZE:]
    return (t1 - s1 * jnp.sum(t1, axis=0, keepdims=True)) - (
        t2 - s2 * jnp.sum(t2, axis=0, keepdims=True)
    )


def with_ones(value):
    tail = lax.broadcasted_iota(jnp.int32, (AUG - HEAD_SIZE, value.shape[1]), 0) == 0
    return jnp.concatenate([value, tail.astype(F32).astype(BF16)], axis=0)


def head_rows(h, size=HEAD_SIZE):
    return slice(h * size, (h + 1) * size)


def features_kernel(heads, groups, qkv_ref, halo_ref, maps_ref, keep_ref, fq_ref, fk_ref, state_ref):
    per = heads // groups
    base = heads * HEAD_SIZE
    keep = keep_ref[0].astype(BF16)
    for g in range(groups):
        rows = slice(base + g * HEAD_SIZE, base + (g + 1) * HEAD_SIZE)
        key = jnp.concatenate([qkv_ref[rows, :], halo_ref[0, head_rows(g), :]], axis=1)
        rows = slice(base + (groups + g) * HEAD_SIZE, base + (groups + g + 1) * HEAD_SIZE)
        value = jnp.concatenate([qkv_ref[rows, :], halo_ref[0, head_rows(groups + g), :]], axis=1)
        value = with_ones(value) * keep
        key_twice = jnp.concatenate([key, key], axis=0)
        for h in range(g * per, (g + 1) * per):
            query = qkv_ref[head_rows(h), :]
            fq_ref[0, head_rows(h, 128), :] = soft_pair(
                nn(maps_ref[0, h], jnp.concatenate([query, query], axis=0))
            )
            feat = soft_pair(nn(maps_ref[1, h], key_twice))
            fk_ref[0, head_rows(h, 128), :] = feat
            state_ref[0, head_rows(h, AUG), :] = nt(value, feat)


def attend_kernel(
    heads,
    groups,
    stretch,
    qkv_ref,
    halo_ref,
    fq_ref,
    fk_ref,
    prior_ref,
    docq_ref,
    dock_ref,
    use_ref,
    attn_ref,
    exact_ref,
    rden_ref,
    weight_ref,
):
    per = heads // groups
    base = heads * HEAD_SIZE
    near, far = masks(docq_ref[0], dock_ref[0], stretch)
    use = use_ref[0]
    for g in range(groups):
        rows = slice(base + g * HEAD_SIZE, base + (g + 1) * HEAD_SIZE)
        key = jnp.concatenate([qkv_ref[rows, :], halo_ref[0, head_rows(g), :]], axis=1)
        rows = slice(base + (groups + g) * HEAD_SIZE, base + (groups + g + 1) * HEAD_SIZE)
        value = jnp.concatenate([qkv_ref[rows, :], halo_ref[0, head_rows(groups + g), :]], axis=1)
        for h in range(g * per, (g + 1) * per):
            query = qkv_ref[head_rows(h), :]
            feat_q = fq_ref[0, head_rows(h, 128), :]
            scores = tn(key, query) * HEAD_SIZE ** (-0.5)
            linear = tn(fk_ref[0, head_rows(h, 128), :], feat_q)
            weight = jnp.where(near, jnp.exp(scores), jnp.where(far, linear, 0.0))
            narrow = weight.astype(BF16)
            weight_ref[0, h] = narrow
            before = nn(prior_ref[0, head_rows(h, AUG), :], feat_q) * use
            total = jnp.sum(weight, axis=0, keepdims=True) + before[HEAD_SIZE : HEAD_SIZE + 1]
            inverse = 1.0 / total
            exact = (nn(value, narrow) + before[:HEAD_SIZE]) * inverse
            exact_ref[0, head_rows(h), :] = exact
            attn_ref[head_rows(h), :] = exact.astype(BF16)
            rden_ref[0, h : h + 1, :] = inverse


def attend_back_kernel(
    heads,
    groups,
    stretch,
    qkv_ref,
    halo_ref,
    fq_ref,
    fk_ref,
    prior_ref,
    docq_ref,
    dock_ref,
    use_ref,
    exact_ref,
    rden_ref,
    weight_ref,
    dattn_ref,
    maps_ref,
    dq_ref,
    dkv_ref,
    dfk_ref,
    dprior_ref,
    dmaps_ref,
):
    per = heads // groups
    base = heads * HEAD_SIZE
    near, far = masks(docq_ref[0], dock_ref[0], stretch)
    use = use_ref[0]
    first_row = lax.broadcasted_iota(jnp.int32, (AUG - HEAD_SIZE, stretch), 0) == 0
    for g in range(groups):
        rows = slice(base + g * HEAD_SIZE, base + (g + 1) * HEAD_SIZE)
        key = jnp.concatenate([qkv_ref[rows, :], halo_ref[0, head_rows(g), :]], axis=1)
        rows = slice(base + (groups + g) * HEAD_SIZE, base + (groups + g + 1) * HEAD_SIZE)
        value = jnp.concatenate([qkv_ref[rows, :], halo_ref[0, head_rows(groups + g), :]], axis=1)
        d_key = jnp.zeros((HEAD_SIZE, stretch + WIN), F32)
        d_value = jnp.zeros((HEAD_SIZE, stretch + WIN), F32)
        for h in range(g * per, (g + 1) * per):
            query = qkv_ref[head_rows(h), :]
            feat_q = fq_ref[0, head_rows(h, 128), :]
            feat_k = fk_ref[0, head_rows(h, 128), :]
            weight = weight_ref[0, h]
            grad = dattn_ref[head_rows(h), :].astype(F32) * rden_ref[0, h : h + 1, :]
            lean = -jnp.sum(grad * exact_ref[0, head_rows(h), :], axis=0, keepdims=True)
            narrow = grad.astype(BF16)
            d_weight = tn(value, narrow) + lean
            d_score = jnp.where(near, d_weight * weight.astype(F32), 0.0).astype(BF16)
            d_linear = jnp.where(far, d_weight, 0.0).astype(BF16)
            both = jnp.concatenate([grad, jnp.where(first_row, lean, 0.0)], axis=0) * use
            both = both.astype(BF16)
            prior = prior_ref[0, head_rows(h, AUG), :]
            dprior_ref[0, head_rows(h, AUG), :] = nt(both, feat_q)
            d_feat = nn(feat_k, d_linear) + tn(prior, both)
            d_proj = soft_pair_back(feat_q, d_feat).astype(BF16)
            d_query = nn(key, d_score) * HEAD_SIZE ** (-0.5) + nn(maps_ref[0, h], d_proj)
            dq_ref[head_rows(h), :] = d_query.astype(BF16)
            dmaps_ref[0, h] = nt(query, d_proj)
            d_key += nt(query, d_score) * HEAD_SIZE ** (-0.5)
            d_value += nt(narrow, weight)
            dfk_ref[0, head_rows(h, 128), :] = nt(feat_q, d_linear).astype(BF16)
        dkv_ref[0, head_rows(g), :] = d_key
        dkv_ref[0, head_rows(groups + g), :] = d_value


def key_back_kernel(
    heads,
    groups,
    qkv_ref,
    halo_ref,
    fk_ref,
    keep_ref,
    dkv_ref,
    dfk_ref,
    dstate_ref,
    maps_ref,
    out_ref,
    dmaps_ref,
):
    per = heads // groups
    base = heads * HEAD_SIZE
    keep = keep_ref[0]
    keep_b = keep.astype(BF16)
    for g in range(groups):
        rows = slice(base + g * HEAD_SIZE, base + (g + 1) * HEAD_SIZE)
        key = jnp.concatenate([qkv_ref[rows, :], halo_ref[0, head_rows(g), :]], axis=1)
        rows = slice(base + (groups + g) * HEAD_SIZE, base + (groups + g + 1) * HEAD_SIZE)
        value = jnp.concatenate([qkv_ref[rows, :], halo_ref[0, head_rows(groups + g), :]], axis=1)
        value = with_ones(value) * keep_b
        d_key = dkv_ref[0, head_rows(g), :]
        d_value = dkv_ref[0, head_rows(groups + g), :]
        for h in range(g * per, (g + 1) * per):
            feat = fk_ref[0, head_rows(h, 128), :]
            d_state = dstate_ref[0, head_rows(h, AUG), :]
            d_feat = dfk_ref[0, head_rows(h, 128), :].astype(F32) + tn(d_state, value)
            d_value += nn(d_state[:HEAD_SIZE], feat) * keep
            d_proj = soft_pair_back(feat, d_feat).astype(BF16)
            d_key += nn(maps_ref[1, h], d_proj)
            dmaps_ref[0, h] = nt(key, d_proj)
        out_ref[0, head_rows(g), :] = d_key
        out_ref[0, head_rows(groups + g), :] = d_value


def lead(*shape):
    rest = (0,) * (len(shape))
    return pl.BlockSpec((1,) + shape, lambda b: (b,) + rest)


def cols(rows, width):
    return pl.BlockSpec((rows, width), lambda b: (0, b))


def fixed(*shape):
    rest = (0,) * len(shape)
    return pl.BlockSpec(shape, lambda b: rest)


def doc_of(starts, positions):
    return jnp.sum((starts[:, None, :] <= positions[None, :, None]).astype(jnp.int32), axis=2) - 1


def per_device(
    activations,
    cotangent,
    document_starts,
    norm_gain_pair,
    query_projection_weight,
    key_value_weight,
    output_projection_weight,
    gate_up_weight,
    down_weight,
    adapter_down_maps,
    query_adapter_up,
    keyval_adapter_up,
    output_adapter_down,
    output_adapter_up,
    hedgehog_maps,
):
    n_seq, n_kv = lax.axis_size("seq"), lax.axis_size("kv")
    me, level = lax.axis_index("seq"), lax.axis_index("kv")
    stretch = activations.shape[1]
    q_cols = query_projection_weight.shape[1]
    kv_cols = key_value_weight.shape[2]
    heads, groups = q_cols // HEAD_SIZE, kv_cols // HEAD_SIZE
    hidden_units = down_weight.shape[0]
    qkv_cols = q_cols + 2 * kv_cols
    keys = stretch + WIN
    share_rows = stretch // n_kv
    shard = norm_gain_pair.shape[1]
    begin = me * stretch
    rank = ADAPTER_RANK

    pack_a = jnp.concatenate(
        [
            query_projection_weight,
            key_value_weight[0],
            key_value_weight[1],
            jnp.pad(
                jnp.concatenate([adapter_down_maps, norm_gain_pair.T], axis=1),
                ((0, 0), (0, 128 - 3 * rank - 2)),
            ),
        ],
        axis=1,
    )
    pack_b = jnp.concatenate(
        [
            output_projection_weight.T,
            jnp.pad(output_adapter_up.T, ((0, 0), (0, 128 - rank))),
        ],
        axis=1,
    )
    pack_c = jnp.concatenate([gate_up_weight[0], gate_up_weight[1]], axis=1)
    by_hops = shard % 128 == 0
    if by_hops:
        pieces_a = second_hops(first_hops(pack_a))
        *pieces_a, pack_b, pack_c, pack_d = together(*pieces_a, pack_b, pack_c, down_weight.T)
        hops_b = first_hops(pack_b)
        full_a = ordered_rows(pieces_a)
    else:
        pack_d = down_weight.T
        full_a = lax.all_gather(pack_a, "seq", axis=0, tiled=True)
    full_d = lax.all_gather(pack_d, "seq", axis=0, tiled=True)
    full_c = lax.all_gather(pack_c, "seq", axis=0, tiled=True)
    gains = full_a[:, qkv_cols + 3 * rank : qkv_cols + 3 * rank + 2].T.astype(F32)
    up_rows = jnp.concatenate(
        [
            jnp.pad(query_adapter_up, ((0, 0), (0, 2 * kv_cols))),
            jnp.pad(keyval_adapter_up[0], ((0, 0), (q_cols, kv_cols))),
            jnp.pad(keyval_adapter_up[1], ((0, 0), (q_cols + kv_cols, 0))),
        ],
        axis=0,
    )

    maps_high = hedgehog_maps.astype(BF16)
    maps_rest = (hedgehog_maps - maps_high.astype(F32)).astype(BF16)
    maps_t = jnp.concatenate(
        [jnp.swapaxes(maps_high, 2, 3), jnp.swapaxes(maps_rest, 2, 3)], axis=3
    )

    pos_q = begin + jnp.arange(stretch, dtype=jnp.int32)
    pos_k = jnp.concatenate([pos_q, begin - WIN + jnp.arange(WIN, dtype=jnp.int32)])
    doc_q = doc_of(document_starts, pos_q)
    doc_k = doc_of(document_starts, pos_k)
    ends = (jnp.arange(-1, n_seq, dtype=jnp.int32) + 1) * stretch - WIN - 1
    doc_ends = doc_of(document_starts, ends)

    def doc_end(k):
        return lax.dynamic_index_in_dim(doc_ends, k + 1, axis=1, keepdims=False)

    doc_prev, doc_last = doc_end(me - 1), doc_end(me)
    keep = (doc_k == doc_last[:, None]) & (pos_k < begin + stretch - WIN)[None, :]
    keep = keep.astype(F32)[:, None, :]
    use = (doc_q == doc_prev[:, None]).astype(F32)[:, None, :]
    doc_q3, doc_k3 = doc_q[:, None, :], doc_k[:, :, None]

    def prefix(value, first):
        m = value.shape[0]
        total, found = value, jnp.zeros_like(value)
        bit = 1
        while bit < n_seq:
            other = flip(total.astype(BF16), "seq", bit).astype(F32)
            upper = (me & bit) != 0
            low_end = (me & ~(2 * bit - 1)) + bit - 1
            low_doc = doc_end(low_end)[first : first + m]
            join = (low_doc == doc_end(low_end + bit)[first : first + m])[:, None, None]
            wanted = ((low_doc == doc_prev[first : first + m]) & upper)[:, None, None]
            found = found + jnp.where(wanted, other, 0.0)
            below, above = jnp.where(upper, other, total), jnp.where(upper, total, other)
            total = above + jnp.where(join, below, 0.0)
            bit *= 2
        return found.astype(BF16)

    def suffix(value, first):
        m = value.shape[0]
        total, found = value, jnp.zeros_like(value)
        bit = 1
        while bit < n_seq:
            other = flip(total.astype(BF16), "seq", bit).astype(F32)
            upper = (me & bit) != 0
            low_first = me & ~(2 * bit - 1)
            high_doc = doc_end(low_first + bit - 1)[first : first + m]
            join = (high_doc == doc_end(low_first - 1)[first : first + m])[:, None, None]
            wanted = ((high_doc == doc_last[first : first + m]) & ~upper)[:, None, None]
            found = found + jnp.where(wanted, other, 0.0)
            below, above = jnp.where(upper, other, total), jnp.where(upper, total, other)
            total = below + jnp.where(join, above, 0.0)
            bit *= 2
        return found.astype(BF16)

    rows_all = MB * stretch
    inputs = activations.reshape(rows_all, MODEL_WIDTH)
    cotangents = cotangent.reshape(rows_all, MODEL_WIDTH)
    inputs_wide = inputs.astype(F32)
    scale_one = lax.rsqrt(jnp.mean(inputs_wide * inputs_wide, axis=1, keepdims=True) + EPSILON)
    normed_one = (inputs_wide * scale_one * gains[0:1]).astype(BF16)

    def own_rows(values):
        chunked = values.reshape(MB, n_kv, share_rows, values.shape[1])
        return lax.dynamic_index_in_dim(chunked, level, axis=1, keepdims=False)

    def by_level(values):
        return values.reshape(MB, n_kv, share_rows, MODEL_WIDTH)

    def padded(rows):
        return jnp.pad(rows, ((0, 128 - rows.shape[0]), (0, 0)))

    whole = tn(full_a, normed_one.T)
    adapt = whole[qkv_cols : qkv_cols + 3 * rank].astype(BF16)
    qkv = (whole[:qkv_cols] + tn(up_rows, adapt)).astype(BF16)
    edge = jnp.stack([qkv[q_cols:, (b + 1) * stretch - WIN : (b + 1) * stretch] for b in range(MB)])
    halo = shift(edge, "seq", 1)
    if by_hops:
        halo, *hops_b = together(halo, *hops_b)
        pieces_b = second_hops(hops_b)
    fq, fk, state = pl.pallas_call(
        functools.partial(features_kernel, heads, groups),
        grid=(MB,),
        in_specs=[
            cols(qkv_cols, stretch),
            lead(2 * kv_cols, WIN),
            fixed(2, heads, HEAD_SIZE, 2 * HEAD_SIZE),
            lead(1, keys),
        ],
        out_specs=[lead(heads * 128, stretch), lead(heads * 128, keys), lead(heads * AUG, 128)],
        out_shape=[
            jax.ShapeDtypeStruct((MB, heads * 128, stretch), BF16),
            jax.ShapeDtypeStruct((MB, heads * 128, keys), BF16),
            jax.ShapeDtypeStruct((MB, heads * AUG, 128), F32),
        ],
        compiler_params=params(1),
        cost_estimate=cost(5),
    )(qkv, halo, maps_t, keep)
    prior = prefix(state, 0)
    if by_hops:
        full_b = ordered_rows(pieces_b)
        full_b, prior = together(full_b, prior)
    else:
        full_b = lax.all_gather(pack_b, "seq", axis=0, tiled=True)
    attn, exact, rden, weight = pl.pallas_call(
        functools.partial(attend_kernel, heads, groups, stretch),
        grid=(MB,),
        in_specs=[
            cols(qkv_cols, stretch),
            lead(2 * kv_cols, WIN),
            lead(heads * 128, stretch),
            lead(heads * 128, keys),
            lead(heads * AUG, 128),
            lead(1, stretch),
            lead(keys, 1),
            lead(1, stretch),
        ],
        out_specs=[
            cols(q_cols, stretch),
            lead(q_cols, stretch),
            lead(heads, stretch),
            lead(heads, keys, stretch),
        ],
        out_shape=[
            jax.ShapeDtypeStruct((q_cols, rows_all), BF16),
            jax.ShapeDtypeStruct((MB, q_cols, stretch), F32),
            jax.ShapeDtypeStruct((MB, heads, stretch), F32),
            jax.ShapeDtypeStruct((MB, heads, keys, stretch), BF16),
        ],
        compiler_params=params(1),
        cost_estimate=cost(7),
    )(qkv, halo, fq, fk, prior, doc_q3, doc_k3, use)
    reduced = tn(output_adapter_down, attn)
    attn_aug = jnp.concatenate([attn, padded(reduced.astype(BF16))], axis=0)
    project = nt(attn_aug.T, full_b).astype(BF16)
    terms = level_send(by_level(project), 1)
    d_hidden = nn(cotangents, full_d).astype(BF16)
    x_own, c_own = own_rows(inputs), own_rows(cotangents)
    *terms, d_hidden, x_own, c_own = together(*terms, d_hidden, x_own, c_own)
    resid = x_own.astype(F32) + total_of(terms)
    pieces = level_spread(resid.astype(BF16))
    resid_all, normed_two = level_rows(pieces, BF16, gains[1:2])

    def weight_gradient(left, right, right_axis):
        return contract(left, right, ((0,), (right_axis,))).astype(BF16)

    def over_seq(part):
        return lax.psum_scatter(part, "seq", scatter_dimension=0, tiled=True)

    hidden, d_gu, d_normed = feed_forward(normed_two, d_hidden, full_c)
    terms = level_send(by_level(d_normed), 1)
    part_cd = wide_gradients(normed_two, d_gu, cotangents, hidden)
    core = me % 2
    first_one, second_one = parity_rows(normed_one, 1 - core), parity_rows(normed_one, core)
    *terms, part_cd, reduced, first_one, second_one = together(
        *terms, part_cd, reduced, first_one, second_one
    )
    grad_cd = over_seq(part_cd)
    d_normed = total_of(terms)
    scale = lax.rsqrt(jnp.mean(resid * resid, axis=2, keepdims=True) + EPSILON)
    gain_two = jnp.sum(d_normed * resid * scale, axis=(0, 1))
    weighted = gains[1] * d_normed
    d_resid = (
        c_own.astype(F32)
        + scale * weighted
        - resid * scale**3 * jnp.mean(weighted * resid, axis=2, keepdims=True)
    )
    pieces = level_spread(d_resid.astype(BF16))
    share = MODEL_WIDTH // n_kv
    down = nt(hidden, full_d).astype(BF16)
    reduce_all = sum_once(reduced, "kv").astype(BF16)
    *pieces, down, reduce_all = together(*pieces, down, reduce_all)
    d_branch = level_rows(pieces, BF16)

    back = tn(full_b, d_branch.T)
    d_reduce = back[q_cols : q_cols + rank].astype(BF16)
    d_attn = (back[:q_cols] + nn(output_adapter_down, d_reduce)).astype(BF16)
    d_attn, down = together(d_attn, down)
    down_terms = level_send(jnp.swapaxes(down.reshape(rows_all, n_kv, share), 0, 1), 0)
    d_query, d_kv, d_fk, d_prior, d_maps_q = pl.pallas_call(
        functools.partial(attend_back_kernel, heads, groups, stretch),
        grid=(MB,),
        in_specs=[
            cols(qkv_cols, stretch),
            lead(2 * kv_cols, WIN),
            lead(heads * 128, stretch),
            lead(heads * 128, keys),
            lead(heads * AUG, 128),
            lead(1, stretch),
            lead(keys, 1),
            lead(1, stretch),
            lead(q_cols, stretch),
            lead(heads, stretch),
            lead(heads, keys, stretch),
            cols(q_cols, stretch),
            fixed(2, heads, HEAD_SIZE, HEAD_SIZE),
        ],
        out_specs=[
            cols(q_cols, stretch),
            lead(2 * kv_cols, keys),
            lead(heads * 128, keys),
            lead(heads * AUG, 128),
            lead(heads, HEAD_SIZE, HEAD_SIZE),
        ],
        out_shape=[
            jax.ShapeDtypeStruct((q_cols, rows_all), BF16),
            jax.ShapeDtypeStruct((MB, 2 * kv_cols, keys), F32),
            jax.ShapeDtypeStruct((MB, heads * 128, keys), BF16),
            jax.ShapeDtypeStruct((MB, heads * AUG, 128), F32),
            jax.ShapeDtypeStruct((MB, heads, HEAD_SIZE, HEAD_SIZE), F32),
        ],
        compiler_params=params(1),
        cost_estimate=cost(13),
    )(
        qkv,
        halo,
        fq,
        fk,
        prior,
        doc_q3,
        doc_k3,
        use,
        exact,
        rden,
        weight,
        d_attn,
        maps_high,
    )
    d_state = suffix(d_prior, 0)
    right_b = jnp.concatenate([attn, padded(reduce_all)], axis=0)
    arrived_b = flip(weight_gradient(parity_rows(d_branch, 1 - core), right_b, 1), "seq", 1)
    kept_b = weight_gradient(parity_rows(d_branch, core), right_b, 1)
    d_state, kept_b = together(d_state, kept_b)
    d_kv, d_maps_k = pl.pallas_call(
        functools.partial(key_back_kernel, heads, groups),
        grid=(MB,),
        in_specs=[
            cols(qkv_cols, stretch),
            lead(2 * kv_cols, WIN),
            lead(heads * 128, keys),
            lead(1, keys),
            lead(2 * kv_cols, keys),
            lead(heads * 128, keys),
            lead(heads * AUG, 128),
            fixed(2, heads, HEAD_SIZE, HEAD_SIZE),
        ],
        out_specs=[lead(2 * kv_cols, keys), lead(heads, HEAD_SIZE, HEAD_SIZE)],
        out_shape=[
            jax.ShapeDtypeStruct((MB, 2 * kv_cols, keys), F32),
            jax.ShapeDtypeStruct((MB, heads, HEAD_SIZE, HEAD_SIZE), F32),
        ],
        compiler_params=params(1),
        cost_estimate=cost(7),
    )(qkv, halo, fk, keep, d_kv, d_fk, d_state, maps_high)
    d_kv, arrived_b, *down_terms = together(d_kv, arrived_b, *down_terms)
    terms_b = chip_pair(kept_b, arrived_b)
    back_edge = shift(d_kv[:, :, stretch:].astype(BF16), "seq", -1).astype(F32)
    d_kv = d_kv[:, :, :stretch] + jnp.pad(back_edge, ((0, 0), (0, 0), (stretch - WIN, 0)))
    d_kv = jnp.concatenate([d_kv[b] for b in range(MB)], axis=1).astype(BF16)
    d_qkv = jnp.concatenate([d_query, d_kv], axis=0)
    d_adapt = nn(up_rows, d_qkv)
    d_qkv_aug = jnp.concatenate([d_qkv, padded(d_adapt.astype(BF16))], axis=0)
    d_normed = nt(d_qkv_aug.T, full_a).astype(BF16)
    block_out = total_of(down_terms) + lax.dynamic_slice_in_dim(
        resid_all, level * share, share, 1
    ).astype(F32)
    block_out = block_out.astype(BF16).reshape(MB, stretch, share)
    terms = level_send(by_level(d_normed), 1)
    d_adapt_all = sum_once(d_adapt, "kv").astype(BF16)
    right_a = jnp.concatenate([d_qkv, padded(d_adapt_all)], axis=0)
    arrived_a = flip(weight_gradient(first_one, right_a, 1), "seq", 1)
    kept_a = weight_gradient(second_one, right_a, 1)
    terms_a = chip_pair(kept_a, arrived_a)
    lora = nt(adapt, d_qkv)
    ready = together(*terms, lora, *terms_b)
    terms, lora, terms_b = ready[:n_kv], ready[n_kv], ready[n_kv + 1 :]
    d_normed = total_of(terms)
    x_own = x_own.astype(F32)
    scale = own_rows(scale_one)
    gain_one = jnp.sum(d_normed * x_own * scale, axis=(0, 1))
    weighted = gains[0] * d_normed
    d_input = (
        d_resid
        + scale * weighted
        - x_own * scale**3 * jnp.mean(weighted * x_own, axis=2, keepdims=True)
    )
    pieces = level_spread(d_input.astype(BF16))

    gain_rows = jnp.stack([gain_one, gain_two])
    grad_gains = scatter_lanes(sum_once(gain_rows, "kv"), "seq")

    grad_lora_q = lora[:rank, :q_cols]
    grad_lora_k = lora[rank : 2 * rank, q_cols : q_cols + kv_cols]
    grad_lora_v = lora[2 * rank :, q_cols + kv_cols :]
    grad_reduce = nt(d_reduce, attn)
    d_maps = jnp.stack([d_maps_q.sum(0), d_maps_k.sum(0)])
    small = [grad_lora_q, grad_lora_k, grad_lora_v, grad_reduce, d_maps]
    sizes = [part.size // 128 for part in small]
    packed = sum_all(jnp.concatenate([part.reshape(-1, 128) for part in small], axis=0), "seq")
    outs, at = [], 0
    for part, size in zip(small, sizes):
        outs.append(packed[at : at + size].reshape(part.shape))
        at += size
    grad_lora_q, grad_lora_k, grad_lora_v, grad_reduce, grad_maps = outs

    ready = together(*pieces, grad_gains, *terms_a)
    pieces, grad_gains, terms_a = ready[:n_kv], ready[n_kv], ready[n_kv + 1 :]
    grad_a, grad_b = total_of(terms_a), total_of(terms_b)
    grad_cd = grad_cd.astype(F32)
    grad_c, grad_d = grad_cd[:, : 2 * hidden_units], grad_cd[:, 2 * hidden_units :]
    grad_enter = grad_a[:, qkv_cols : qkv_cols + 3 * rank]
    grad_expand = grad_b[:, q_cols : q_cols + rank].T
    grad_input = level_rows(pieces, F32).reshape(MB, stretch, MODEL_WIDTH)

    return (
        block_out,
        grad_input,
        grad_gains,
        grad_a[:, :q_cols],
        jnp.stack([grad_a[:, q_cols : q_cols + kv_cols], grad_a[:, q_cols + kv_cols : qkv_cols]]),
        grad_b[:, :q_cols].T,
        jnp.stack([grad_c[:, :hidden_units], grad_c[:, hidden_units:]]),
        grad_d.T,
        grad_enter,
        grad_lora_q,
        jnp.stack([grad_lora_k, grad_lora_v]),
        grad_reduce.T,
        grad_expand,
        grad_maps,
    )


def solution(mesh):
    placed = (
        P(None, "seq", None),
        P(None, "seq", None),
        P(),
        P(None, "seq"),
        P("seq", "kv"),
        P(None, "seq", "kv"),
        P("kv", "seq"),
        P(None, "seq", "kv"),
        P("kv", "seq"),
        P("seq", None),
        P(None, "kv"),
        P(None, None, "kv"),
        P("kv", None),
        P(None, "seq"),
        P(None, "kv", None, None),
    )
    return jax.shard_map(
        per_device,
        mesh=mesh,
        in_specs=placed,
        out_specs=(
            P(None, "seq", "kv"),
            P(None, "seq", None),
            P(None, "seq"),
            P("seq", "kv"),
            P(None, "seq", "kv"),
            P("kv", "seq"),
            P(None, "seq", "kv"),
            P("kv", "seq"),
            P("seq", None),
            P(None, "kv"),
            P(None, None, "kv"),
            P("kv", None),
            P(None, "seq"),
            P(None, "kv", None, None),
        ),
        check_vma=False,
    )
```
